32 devices in a mesh: seq: 16 (over z, y, x), head: 2 (over core).
Axes of the slice: x: 2, y: 2, z: 4, core: 2. Of those that a mesh axis runs over, the one named last changes fastest.
Arguments:
- queries: bfloat16 [8192, 1024], P('seq', 'head'), may hold values from -12 to 12
- key_states: bfloat16 [8192, 1024], P('seq', 'head'), may hold values from -5 to 5
- value_states: bfloat16 [8192, 1024], P('seq', 'head'), may hold values from -6 to 6
- out_grad: bfloat16 [8192, 1024], P('seq', 'head'), may hold values from -6 to 6
Outputs:
- normalized: bfloat16 [8192, 1024], P('seq', 'head')
- grad_queries: bfloat16 [8192, 1024], P('seq', 'head')
- grad_keys: bfloat16 [8192, 1024], P('seq', 'head')
- grad_values: bfloat16 [8192, 1024], P('seq', 'head')
The draws below stay inside these ranges and needn't reach their ends.
All inputs are finite; a program needn't handle non-finite values.
Results may differ from the reference program's by a relative error of at most 0.035.
Values may be sent and summed in bfloat16 or wider, within the bound.
A program may use at most 64 MiB of HBM per device.

```python
from functools import reduce
import jax
import jax.numpy as jnp
from jax import lax

DH = 128
HEADS = 8
LEAF = 256
LEVELS = 3
TOKENS = 8192


def draw_queries(key, part):
    noise = jax.random.truncated_normal(jax.random.fold_in(key, 1), -4.0, 4.0, (TOKENS, HEADS * DH), jnp.float32)
    return noise.astype(jnp.bfloat16)


def draw_key_states(key, part):
    noise = jax.random.truncated_normal(jax.random.fold_in(key, 2), -4.0, 4.0, (TOKENS, HEADS * DH), jnp.float32)
    return noise.astype(jnp.bfloat16)


def draw_value_states(key, part):
    head_of = (jnp.arange(HEADS * DH) // DH).astype(jnp.float32) / (HEADS - 1)
    noise = jax.random.truncated_normal(jax.random.fold_in(key, 3), -4.0, 4.0, (TOKENS, HEADS * DH), jnp.float32)
    scaled = noise * (0.5 * 3.0 ** head_of)[None, :]
    return scaled.astype(jnp.bfloat16)


def levels(own_key, shape, cuts, least, largest):
    gain = 1.0
    for dim, shards_of in cuts:
        steps = jax.random.uniform(jax.random.fold_in(jax.random.fold_in(own_key, 6), dim), (shards_of,), jnp.float32, least / len(cuts), largest / len(cuts))
        gain = gain * jnp.repeat(jnp.exp(steps), shape[dim] // shards_of).reshape((-1,) + (1,) * (len(shape) - 1 - dim))
    return gain


def centred(own_key, extent, width, bound, shards=(), kind=jnp.bfloat16):
    loudness = levels(own_key, extent, shards, -0.22, 0.18) if shards else 1.0
    entries = jax.random.normal(own_key, extent, jnp.float32) * width * loudness
    return jnp.minimum(jnp.maximum(entries, -bound), bound).astype(kind)


def setup_inputs(seed: int = 0) -> dict:
    key_list = jax.random.split(jax.random.key(seed), 5)
    return {
        "queries": draw_queries(jax.random.fold_in(key_list[4], 71), 0),
        "key_states": draw_key_states(jax.random.fold_in(key_list[4], 71), 0),
        "value_states": draw_value_states(jax.random.fold_in(key_list[4], 71), 0),
        "out_grad": centred(key_list[3], (TOKENS, HEADS * DH), 1.0, 6.0, ((0, 16), (1, 2))),
    }


EPSILON = 1e-06

def halving(source):
    widened = source.astype(jnp.float32)
    paired = widened.reshape(widened.shape[:-2] + (widened.shape[-2] // 2, 2, widened.shape[-1]))
    return ((paired[..., 0, :] + paired[..., 1, :]) * 0.5).astype(jnp.bfloat16)

def query_view(tensor, level_num):
    flat_width = tensor.shape[-1]
    if level_num == 0:
        return tensor.reshape(-1, 2 * LEAF, flat_width)
    return tensor.reshape(-1, LEAF, flat_width)

def key_view(tensor, level_num):
    flat_width = tensor.shape[-1]
    if level_num == 0:
        return tensor.reshape(-1, 2 * LEAF, flat_width)
    return jnp.flip(tensor.reshape(-1, 2, LEAF, flat_width), 1).reshape(-1, LEAF, flat_width)

def key_rows(blocks, level_num):
    flat_width = blocks.shape[-1]
    if level_num == 0:
        return blocks.reshape(-1, flat_width)
    return jnp.flip(blocks.reshape(-1, 2, LEAF, flat_width), 1).reshape(-1, flat_width)

def coarse_all(tensor):
    result = [tensor]
    for level_num in range(1, LEVELS):
        result.append(halving(result[-1]))
    return result

def level_scores(coarse_query, coarse_key, level_num):
    query_blocks = query_view(coarse_query[level_num], level_num).astype(jnp.float32)
    key_blocks = key_view(coarse_key[level_num], level_num).astype(jnp.float32)
    scores = jnp.einsum('gqd,gkd->gqk', query_blocks, key_blocks) * DH ** (-0.5)
    maxima = scores.max(-1)
    exp_scores = jnp.exp(scores - maxima[..., None])
    return (query_blocks, key_blocks, maxima, exp_scores)

def head_attention(head_query, head_key, head_value):
    coarse_query = coarse_all(head_query)
    coarse_key = coarse_all(head_key)
    coarse_value = coarse_all(head_value)
    maxima_up, sums_up, weighted_up = ([], [], [])
    for level_num in range(LEVELS):
        stretch = 2 ** level_num
        query_blocks, key_blocks, maxima, exp_scores = level_scores(coarse_query, coarse_key, level_num)
        rounded = lax.optimization_barrier(exp_scores.astype(jnp.bfloat16)).astype(jnp.float32)
        value_blocks = key_view(coarse_value[level_num], level_num).astype(jnp.float32)
        weighted = jnp.einsum('gqk,gkd->gqd', rounded, value_blocks)
        maxima_up.append(jnp.repeat(maxima.reshape(-1), stretch, axis=0))
        sums_up.append(jnp.repeat(exp_scores.sum(-1).reshape(-1), stretch, axis=0))
        weighted_up.append(jnp.repeat(weighted.reshape(-1, DH), stretch, axis=0))
    highest = reduce(jnp.maximum, maxima_up)
    factors = [2.0 ** level_num * jnp.exp(maxima_up[level_num] - highest) for level_num in range(LEVELS)]
    denominator = factors[0] * sums_up[0]
    numerator = factors[0][:, None] * weighted_up[0]
    for level_num in range(1, LEVELS):
        denominator = denominator + factors[level_num] * sums_up[level_num]
        numerator = numerator + factors[level_num][:, None] * weighted_up[level_num]
    attended = (numerator / denominator[:, None]).astype(jnp.bfloat16)
    return (attended, factors, denominator)

def head_backward(head_query, head_key, head_value, head_grad):
    attended, factors, denominator = head_attention(head_query, head_key, head_value)
    coarse_query = coarse_all(head_query)
    coarse_key = coarse_all(head_key)
    coarse_value = coarse_all(head_value)
    attended_wide = attended.astype(jnp.float32)
    row_dots = lax.optimization_barrier(jnp.sum(head_grad * attended_wide, axis=-1))
    grad_total = jnp.zeros((3,) + head_query.shape, jnp.float32)
    for level_num in range(LEVELS):
        stretch = 2 ** level_num
        coarse_rows = head_query.shape[0] // stretch
        share_of = factors[level_num] / denominator
        gathered_grad = (share_of[:, None] * head_grad).reshape(coarse_rows, stretch, DH).sum(1)
        delta_rows = (share_of * row_dots).reshape(coarse_rows, stretch).sum(1)
        query_blocks, key_blocks, maxima, exp_scores = level_scores(coarse_query, coarse_key, level_num)
        rounded = lax.optimization_barrier(exp_scores.astype(jnp.bfloat16)).astype(jnp.float32)
        value_blocks = key_view(coarse_value[level_num], level_num).astype(jnp.float32)
        grad_rounded = lax.optimization_barrier(gathered_grad.astype(jnp.bfloat16)).astype(jnp.float32)
        grad_blocks = query_view(grad_rounded, level_num)
        delta_blocks = delta_rows.reshape(grad_blocks.shape[0], grad_blocks.shape[1])
        grad_scores = jnp.einsum('gqd,gkd->gqk', grad_blocks, value_blocks)
        grad_logits = (exp_scores * (grad_scores - delta_blocks[..., None])).astype(jnp.bfloat16)
        grad_logits = lax.optimization_barrier(grad_logits).astype(jnp.float32)
        grad_query = jnp.einsum('gqk,gkd->gqd', grad_logits, key_blocks) * DH ** (-0.5)
        grad_key = jnp.einsum('gqk,gqd->gkd', grad_logits, query_blocks) * DH ** (-0.5)
        grad_value = jnp.einsum('gqk,gqd->gkd', rounded, grad_blocks)
        level_grads = jnp.stack([grad_query.reshape(-1, DH), key_rows(grad_key, level_num), key_rows(grad_value, level_num)])
        grad_total = grad_total + jnp.repeat(level_grads, stretch, axis=1) * 0.5 ** level_num
    return grad_total

def reference(queries, key_states, value_states, out_grad):
    token_count, full_width = queries.shape
    head_count = full_width // DH

    def by_head(tensor):
        return tensor.reshape(token_count, head_count, DH).transpose(1, 0, 2)

    def forward_head(triple):
        return head_attention(triple[0], triple[1], triple[2])[0]
    attended = lax.map(forward_head, (by_head(queries), by_head(key_states), by_head(value_states)))
    attended = attended.transpose(1, 0, 2).reshape(token_count, full_width)
    attended_wide = attended.astype(jnp.float32)
    inverse = lax.rsqrt(lax.optimization_barrier(jnp.sum(attended_wide * attended_wide, axis=-1)) / full_width + EPSILON)
    normalized = (attended_wide * inverse[:, None]).astype(jnp.bfloat16)
    grad_wide = out_grad.astype(jnp.float32)
    dot_totals = lax.optimization_barrier(jnp.sum(grad_wide * attended_wide, axis=-1))
    grad_attended = inverse[:, None] * grad_wide - (inverse ** 3 * dot_totals / full_width)[:, None] * attended_wide

    def backward_head(quad):
        return head_backward(quad[0], quad[1], quad[2], quad[3])
    grads = lax.map(backward_head, (by_head(queries), by_head(key_states), by_head(value_states), by_head(grad_attended)))
    grads = grads.transpose(1, 2, 0, 3).reshape(3, token_count, full_width).astype(jnp.bfloat16)
    return (normalized, grads[0], grads[1], grads[2])
```

```python
import functools

import jax
import jax.numpy as jnp
from jax import lax
from jax.experimental import pallas as pl
from jax.experimental.pallas import tpu as pltpu
from jax.sharding import PartitionSpec as P

DH = 128
LEAF = 256
EPSILON = 1e-06
SCALE = DH ** (-0.5)
LOG2 = SCALE * 1.4426950408889634
MESH = pl.DeviceIdType.MESH
F32 = jnp.float32
BF16 = jnp.bfloat16
PACK = DH + 16


def nn(a, b):
    return lax.dot_general(a, b, (((1,), (0,)), ((), ())), preferred_element_type=F32)


def nt(a, b):
    return lax.dot_general(a, b, (((1,), (1,)), ((), ())), preferred_element_type=F32)


def wide(x):
    return x.astype(F32)


def flip(x):
    return wide(x).T.astype(BF16)


def halve(x):
    half = x.shape[0] // 2
    return ((wide(x[:half]) + wide(x[half:])) * 0.5).astype(BF16)


def twice(x, axis):
    return jnp.concatenate([x, x], axis)


def fold(x):
    half = x.shape[1] // 2
    return x[:, :half] + x[:, half:]


def packed_rows(first, second, third):
    row = lax.broadcasted_iota(jnp.int32, (16, first.shape[1]), 0)
    return jnp.where(row == 0, first, jnp.where(row == 1, second, jnp.where(row == 2, third, 0.0))).astype(BF16)


def kernel(
    q_ref, k_ref, v_ref, g_ref,
    no_ref, gq_ref, gk_ref, gv_ref,
    perm, back, qs, ks, vs, kts, vts, dos, p0, p1, p2, a0, a1, rows, att,
    q1, kv1, kv1p, k2c, v2c, q2, q2v, a2o, a2i, xo, xi,
    g0, g1, g2o, g2i, dq1, dq2o, dq2i, dkvo, dkvi, dkv0, dkv2,
    send, recv,
):
    tokens, width = q_ref.shape
    heads = width // DH
    half, quarter = tokens // 2, tokens // 4
    full_width = width * 2
    seq, core = lax.axis_index("seq"), lax.axis_index("head")
    at_x = (seq + 1 - 2 * (seq % 2), core)
    at_y = (seq + 2 - 4 * ((seq // 2) % 2), core)
    at_core = (seq, 1 - core)

    def copy(kind, h, source, target, where):
        return pltpu.make_async_remote_copy(
            src_ref=source, dst_ref=target, send_sem=send.at[kind, h], recv_sem=recv.at[kind, h],
            device_id=where, device_id_type=MESH,
        )

    def kv_copy(h):
        return copy(0, h, kv1.at[h], kv1p.at[h], at_x)

    def q2_copy(h):
        return copy(1, h, q2.at[h], q2v.at[h], at_y)

    def a2_copy(h):
        return copy(2, h, a2o.at[h], a2i.at[h], at_y)

    def g2_copy(h):
        return copy(3, h, g2o.at[h], g2i.at[h], at_y)

    def dkv_copy(h):
        return copy(4, h, dkvo.at[h], dkvi.at[h], at_x)

    def dq2_copy(h):
        return copy(5, h, dq2o.at[h], dq2i.at[h], at_y)

    def x_copy():
        return copy(6, 0, xo, xi, at_core)

    def cols(h):
        return pl.ds(pl.multiple_of(h * DH, DH), DH)

    def each_head(body):
        @pl.loop(0, heads)
        def _(h):
            body(h)

    barrier = pltpu.get_barrier_semaphore()
    for where in (at_x, at_y, at_core):
        pl.semaphore_signal(barrier, inc=1, device_id=where, device_id_type=MESH)

    def order(p):
        slab = p // quarter
        return 4 * (p % quarter) + slab // 2 + 2 * (slab % 2)

    shape = (tokens, tokens)
    major = lax.broadcasted_iota(jnp.int32, shape, 0)
    minor = lax.broadcasted_iota(jnp.int32, shape, 1)
    perm[...] = jnp.where(order(major) == minor, 1.0, 0.0).astype(BF16)
    pl.semaphore_wait(barrier, 3)

    def load_kv(h):
        for n, (ref, kept) in enumerate(((k_ref, ks), (v_ref, vs))):
            moved = nn(perm[...], ref[:, cols(h)])
            kept[h] = moved.astype(BF16)
            kv1[h, n] = halve(moved)
        kv_copy(h).start()

    each_head(load_kv)

    def load_q(h):
        moved = nn(perm[...], q_ref[:, cols(h)])
        qs[h] = moved.astype(BF16)
        first = halve(moved)
        q1[h] = first
        q2[h] = halve(first)
        q2_copy(h).start()

    each_head(load_q)

    def softmax(scores):
        top = jnp.max(scores, axis=0, keepdims=True)
        e = jnp.exp2((scores - top) * LOG2)
        return top * LOG2, jnp.sum(e, axis=0, keepdims=True), e.astype(BF16)

    def level0(h):
        kts[h] = flip(ks[h])
        vt = flip(vs[h])
        m, s, p = softmax(nt(ks[h], qs[h]))
        p0[h] = p
        a0[h] = nn(vt, p)
        rows[h, 0:1, :] = m
        rows[h, 1:2, :] = s
        dos[h] = nn(perm[...], g_ref[:, cols(h)]).T.astype(BF16)

    each_head(level0)
    back[...] = jnp.where(order(minor) == major, 1.0, 0.0).astype(BF16)

    def coarse(h):
        kv_copy(h).wait_recv()
        q2_copy(h).wait_recv()
        k1p, v1p = kv1p[h, 0], kv1p[h, 1]
        k2 = jnp.concatenate([halve(kv1[h, 0]), halve(k1p)], 0)
        v2 = jnp.concatenate([halve(kv1[h, 1]), halve(v1p)], 0)
        k2c[h] = k2
        v2c[h] = v2
        scores = nt(k2, q2v[h]) * LOG2
        m = wide(jnp.max(scores, axis=0, keepdims=True).astype(BF16))
        e = jnp.exp2(scores - m)
        s = jnp.sum(e, axis=0, keepdims=True)
        p = e.astype(BF16)
        p2[h] = p
        a2o[h, 0:DH] = nn(flip(v2), p).astype(BF16)
        high = wide(s.astype(BF16))
        a2o[h, DH:PACK] = packed_rows(m, high, s - high)
        a2_copy(h).start()
        m, s, p = softmax(nt(k1p, q1[h]))
        p1[h] = p
        a1[h] = nn(flip(v1p), p)
        rows[h, 2:3, :] = twice(m, 1)
        rows[h, 3:4, :] = twice(s, 1)

    def combine(h):
        a2_copy(h).wait_recv()
        m0, s0 = rows[h, 0:1, :], rows[h, 1:2, :]
        m1, s1 = rows[h, 2:3, :], rows[h, 3:4, :]
        figures = wide(a2i[h, DH:PACK])
        m2 = twice(twice(figures[0:1], 1), 1)
        s2 = twice(twice(figures[1:2] + figures[2:3], 1), 1)
        top = jnp.maximum(jnp.maximum(m0, m1), m2)
        f0 = jnp.exp2(m0 - top)
        f1 = 2.0 * jnp.exp2(m1 - top)
        f2 = 4.0 * jnp.exp2(m2 - top)
        den = 1.0 / (f0 * s0 + f1 * s1 + f2 * s2)
        w0, w1, w2 = f0 * den, f1 * den, f2 * den
        a2 = wide(a2i[h, 0:DH])
        attended = w0 * a0[h] + w1 * twice(a1[h], 1) + w2 * twice(twice(a2, 1), 1)
        rounded = attended.astype(BF16)
        att[h] = rounded
        attended = wide(rounded)
        rows[h, 0:1, :] = w0
        rows[h, 1:2, :] = w1
        rows[h, 2:3, :] = w2
        squares = jnp.sum(attended * attended, axis=0, keepdims=True)
        dots = jnp.sum(attended * wide(dos[h]), axis=0, keepdims=True)
        rows[h, 3:4, :] = squares
        rows[h, 4:5, :] = dots
        xo[0:1, :] += squares
        xo[1:2, :] += dots

    xo[...] = jnp.zeros_like(xo)
    coarse(0)

    @pl.loop(1, heads)
    def _(h):
        coarse(h)
        combine(h - 1)

    combine(heads - 1)
    x_copy().start()
    x_copy().wait_recv()
    inverse = lax.rsqrt((xo[0:1, :] + xi[0:1, :]) / full_width + EPSILON)
    pull = inverse * inverse * inverse * (xo[1:2, :] + xi[1:2, :]) / full_width

    def cotangents(h):
        w0, w1, w2 = rows[h, 0:1, :], rows[h, 1:2, :], rows[h, 2:3, :]
        grad = inverse * wide(dos[h]) - pull * wide(att[h])
        along = inverse * rows[h, 4:5, :] - pull * rows[h, 3:4, :]
        g2o[h, 0:DH] = fold(fold(w2 * grad)).astype(BF16)
        delta = fold(fold(w2 * along))
        high = wide(delta.astype(BF16))
        g2o[h, DH:PACK] = packed_rows(high, delta - high, delta * 0.0)
        g2_copy(h).start()
        g0[h] = (w0 * grad).astype(BF16)
        g1[h] = fold(w1 * grad).astype(BF16)
        rows[h, 5:6, :] = w0 * along
        rows[h, 6:7, :] = twice(fold(w1 * along), 1)

    each_head(cotangents)

    def score_grads(p, values, grads, delta):
        return (wide(p) * (nn(values, grads) - delta)).astype(BF16)

    def coarse_back(h):
        k1p, v1p = kv1p[h, 0], kv1p[h, 1]
        ds = score_grads(p1[h], v1p, g1[h], rows[h, 6:7, 0:half])
        dk = nn(ds, q1[h])
        dv = nt(p1[h], g1[h])
        dq1[h] = nn(flip(k1p), ds)
        g2_copy(h).wait_recv()
        figures = wide(g2i[h, DH:PACK])
        grads = g2i[h, 0:DH]
        ds = score_grads(p2[h], v2c[h], grads, figures[0:1] + figures[1:2])
        dk2 = nn(ds, q2v[h])
        dv2 = nt(p2[h], grads)
        dq2o[h] = nn(flip(k2c[h]), ds).astype(BF16)
        dq2_copy(h).start()
        dkvo[h, 0] = ((dk + 0.5 * twice(dk2[quarter:], 0)) * SCALE).astype(BF16)
        dkvo[h, 1] = (dv + 0.5 * twice(dv2[quarter:], 0)).astype(BF16)
        dkv_copy(h).start()
        dkv2[h, 0] = dk2[:quarter] * SCALE
        dkv2[h, 1] = dv2[:quarter]

    each_head(coarse_back)

    def level0_back(h):
        no_ref[:, cols(h)] = nt(back[...], (wide(att[h]) * inverse).astype(BF16)).astype(BF16)
        ds = score_grads(p0[h], vs[h], g0[h], rows[h, 5:6, :])
        dkv0[h, 0] = nn(ds, qs[h]) * SCALE
        dkv0[h, 1] = nt(p0[h], g0[h])
        dq = nn(kts[h], ds) + 0.5 * twice(dq1[h], 1)
        dq2_copy(h).wait_recv()
        dq = (dq + 0.25 * twice(twice(wide(dq2i[h]), 1), 1)) * SCALE
        gq_ref[:, cols(h)] = nt(back[...], dq.astype(BF16)).astype(BF16)

    each_head(level0_back)

    def finish(h):
        dkv_copy(h).wait_recv()
        for n, out in enumerate((gk_ref, gv_ref)):
            total = (
                dkv0[h, n] + 0.5 * twice(wide(dkvi[h, n]), 0) + 0.25 * twice(twice(dkv2[h, n], 0), 0)
            )
            out[:, cols(h)] = nn(back[...], total.astype(BF16)).astype(BF16)

    each_head(finish)

    def drain(h):
        for make in (kv_copy, q2_copy, a2_copy, g2_copy, dkv_copy, dq2_copy):
            make(h).wait_send()

    each_head(drain)
    x_copy().wait_send()


def shards(queries, key_states, value_states, out_grad):
    tokens, width = queries.shape
    heads = width // DH
    half, quarter = tokens // 2, tokens // 4

    def vmem(*shape, dtype=BF16):
        return pltpu.VMEM(shape, dtype)

    scratch = [
        vmem(tokens, tokens), vmem(tokens, tokens),
        vmem(heads, tokens, DH), vmem(heads, tokens, DH), vmem(heads, tokens, DH),
        vmem(heads, DH, tokens), vmem(heads, DH, tokens), vmem(heads, DH, tokens),
        vmem(heads, tokens, tokens), vmem(heads, half, half), vmem(heads, half, quarter),
        vmem(heads, DH, tokens, dtype=F32), vmem(heads, DH, half, dtype=F32),
        vmem(heads, 8, tokens, dtype=F32), vmem(heads, DH, tokens),
        vmem(heads, half, DH), vmem(heads, 2, half, DH), vmem(heads, 2, half, DH),
        vmem(heads, half, DH), vmem(heads, half, DH),
        vmem(heads, quarter, DH), vmem(heads, quarter, DH),
        vmem(heads, PACK, quarter), vmem(heads, PACK, quarter),
        vmem(8, tokens, dtype=F32), vmem(8, tokens, dtype=F32),
        vmem(heads, DH, tokens), vmem(heads, DH, half),
        vmem(heads, PACK, quarter), vmem(heads, PACK, quarter),
        vmem(heads, DH, half, dtype=F32),
        vmem(heads, DH, quarter), vmem(heads, DH, quarter),
        vmem(heads, 2, half, DH), vmem(heads, 2, half, DH),
        vmem(heads, 2, tokens, DH, dtype=F32), vmem(heads, 2, quarter, DH, dtype=F32),
        pltpu.SemaphoreType.DMA((7, heads)),
        pltpu.SemaphoreType.DMA((7, heads)),
    ]
    flops = 2 * heads * DH * tokens * tokens * 12
    return pl.pallas_call(
        kernel,
        out_shape=[jax.ShapeDtypeStruct((tokens, width), BF16)] * 4,
        in_specs=[pl.BlockSpec(memory_space=pltpu.VMEM)] * 4,
        out_specs=[pl.BlockSpec(memory_space=pltpu.VMEM)] * 4,
        scratch_shapes=scratch,
        compiler_params=pltpu.CompilerParams(
            collective_id=0, has_side_effects=True, vmem_limit_bytes=48 * 1024 * 1024
        ),
        cost_estimate=pl.CostEstimate(
            flops=flops, bytes_accessed=16 * tokens * width, transcendentals=heads * tokens * tokens
        ),
        name="hierarchical_attention",
    )(queries, key_states, value_states, out_grad)


def solution(mesh):
    return jax.shard_map(
        shards,
        mesh=mesh,
        in_specs=(P("seq", "head"),) * 4,
        out_specs=(P("seq", "head"),) * 4,
        check_vma=False,
    )
```

```python
import functools

import jax
import jax.numpy as jnp
from jax import lax
from jax.experimental import pallas as pl
from jax.experimental.pallas import tpu as pltpu
from jax.sharding import PartitionSpec as P

DH = 128
LEAF = 256
EPSILON = 1e-06
SCALE = DH ** (-0.5)
LOG2 = SCALE * 1.4426950408889634
MESH = pl.DeviceIdType.MESH
F32 = jnp.float32
BF16 = jnp.bfloat16
PIECES = 4
VMEM = 60 * 1024 * 1024
PACK = DH + 16


def nn(a, b):
    return lax.dot_general(a, b, (((1,), (0,)), ((), ())), preferred_element_type=F32)


def nt(a, b):
    return lax.dot_general(a, b, (((1,), (1,)), ((), ())), preferred_element_type=F32)


def wide(x):
    return x.astype(F32)


def flip(x):
    return wide(x).T.astype(BF16)


def halve(x):
    half = x.shape[0] // 2
    return ((wide(x[:half]) + wide(x[half:])) * 0.5).astype(BF16)


def twice(x, axis):
    return jnp.concatenate([x, x], axis)


def fold(x):
    half = x.shape[1] // 2
    return x[:, :half] + x[:, half:]


def packed_rows(first, second, third):
    row = lax.broadcasted_iota(jnp.int32, (16, first.shape[1]), 0)
    return jnp.where(row == 0, first, jnp.where(row == 1, second, jnp.where(row == 2, third, 0.0))).astype(BF16)


def kernel(
    q_ref, k_ref, v_ref, g_ref,
    no_ref, gq_ref, gk_ref, gv_ref,
    outs,
    inq, ink, inv, ing, perm, back, qs, ks, vs, kts, vts, dos, p0, p1, p2, a0, a1, rows, att,
    q1, kv1, kv1p, k2c, v2c, q2, q2v, a2o, a2i, xo, xi,
    g0, g1, g2o, g2i, dq1, dq2o, dq2i, dkvo, dkvi, dkv0, dkv2,
    send, recv, arrived, written,
):
    tokens, width = q_ref.shape
    heads = width // DH
    half, quarter = tokens // 2, tokens // 4
    full_width = width * 2
    seq, core = lax.axis_index("seq"), lax.axis_index("head")
    at_x = (seq + 1 - 2 * (seq % 2), core)
    at_y = (seq + 2 - 4 * ((seq // 2) % 2), core)
    at_core = (seq, 1 - core)

    def copy(kind, h, source, target, where):
        return pltpu.make_async_remote_copy(
            src_ref=source, dst_ref=target, send_sem=send.at[kind, h], recv_sem=recv.at[kind, h],
            device_id=where, device_id_type=MESH,
        )

    def kv_copy(h):
        return copy(0, h, kv1.at[h], kv1p.at[h], at_x)

    def q2_copy(h):
        return copy(1, h, q2.at[h], q2v.at[h], at_y)

    def a2_copy(h):
        return copy(2, h, a2o.at[h], a2i.at[h], at_y)

    def g2_copy(h):
        return copy(3, h, g2o.at[h], g2i.at[h], at_y)

    def dkv_copy(h):
        return copy(4, h, dkvo.at[h], dkvi.at[h], at_x)

    def dq2_copy(h):
        return copy(5, h, dq2o.at[h], dq2i.at[h], at_y)

    def x_copy():
        return copy(6, 0, xo, xi, at_core)

    def cols(h):
        return pl.ds(pl.multiple_of(h * DH, DH), DH)

    def each_head(body):
        @pl.loop(0, heads)
        def _(h):
            body(h)

    def fetch(n, h):
        source, target = ((k_ref, ink), (v_ref, inv), (q_ref, inq), (g_ref, ing))[n]
        return pltpu.make_async_copy(source.at[:, cols(h)], target.at[h], arrived.at[n, h])

    def put(n, h):
        target = (no_ref, gq_ref, gk_ref, gv_ref)[n]
        return pltpu.make_async_copy(outs.at[n, h], target.at[:, cols(h)], written.at[n, h])

    barrier = pltpu.get_barrier_semaphore()
    for where in (at_x, at_y, at_core):
        pl.semaphore_signal(barrier, inc=1, device_id=where, device_id_type=MESH)

    for group in ((0, 1), (2, 3)):
        for h in range(heads):
            for n in group:
                fetch(n, h).start()

    def order(p):
        slab = p // quarter
        return 4 * (p % quarter) + slab // 2 + 2 * (slab % 2)

    shape = (tokens, tokens)
    major = lax.broadcasted_iota(jnp.int32, shape, 0)
    minor = lax.broadcasted_iota(jnp.int32, shape, 1)
    perm[...] = jnp.where(order(major) == minor, 1.0, 0.0).astype(BF16)
    pl.semaphore_wait(barrier, 3)

    def load_kv(h):
        for n, (ref, kept) in enumerate(((ink, ks), (inv, vs))):
            fetch(n, h).wait()
            moved = nn(perm[...], ref[h])
            kept[h] = moved.astype(BF16)
            kv1[h, n] = halve(moved)
        kv_copy(h).start()

    each_head(load_kv)

    def load_q(h):
        fetch(2, h).wait()
        moved = nn(perm[...], inq[h])
        qs[h] = moved.astype(BF16)
        first = halve(moved)
        q1[h] = first
        q2[h] = halve(first)
        q2_copy(h).start()

    each_head(load_q)

    def softmax(scores):
        top = jnp.max(scores, axis=0, keepdims=True)
        e = jnp.exp2((scores - top) * LOG2)
        return top * LOG2, jnp.sum(e, axis=0, keepdims=True), e.astype(BF16)

    def level0(h):
        kts[h] = flip(ks[h])
        vt = flip(vs[h])
        m, s, p = softmax(nt(ks[h], qs[h]))
        p0[h] = p
        a0[h] = nn(vt, p)
        rows[h, 0:1, :] = m
        rows[h, 1:2, :] = s
        fetch(3, h).wait()
        dos[h] = nn(perm[...], ing[h]).T.astype(BF16)

    each_head(level0)
    back[...] = jnp.where(order(minor) == major, 1.0, 0.0).astype(BF16)

    def coarse(h):
        kv_copy(h).wait_recv()
        q2_copy(h).wait_recv()
        k1p, v1p = kv1p[h, 0], kv1p[h, 1]
        k2 = jnp.concatenate([halve(kv1[h, 0]), halve(k1p)], 0)
        v2 = jnp.concatenate([halve(kv1[h, 1]), halve(v1p)], 0)
        k2c[h] = k2
        v2c[h] = v2
        scores = nt(k2, q2v[h]) * LOG2
        m = wide(jnp.max(scores, axis=0, keepdims=True).astype(BF16))
        e = jnp.exp2(scores - m)
        s = jnp.sum(e, axis=0, keepdims=True)
        p = e.astype(BF16)
        p2[h] = p
        a2o[h, 0:DH] = nn(flip(v2), p).astype(BF16)
        high = wide(s.astype(BF16))
        a2o[h, DH:PACK] = packed_rows(m, high, s - high)
        a2_copy(h).start()
        m, s, p = softmax(nt(k1p, q1[h]))
        p1[h] = p
        a1[h] = nn(flip(v1p), p)
        rows[h, 2:3, :] = twice(m, 1)
        rows[h, 3:4, :] = twice(s, 1)

    def combine(h):
        a2_copy(h).wait_recv()
        m0, s0 = rows[h, 0:1, :], rows[h, 1:2, :]
        m1, s1 = rows[h, 2:3, :], rows[h, 3:4, :]
        figures = wide(a2i[h, DH:PACK])
        m2 = twice(twice(figures[0:1], 1), 1)
        s2 = twice(twice(figures[1:2] + figures[2:3], 1), 1)
        top = jnp.maximum(jnp.maximum(m0, m1), m2)
        f0 = jnp.exp2(m0 - top)
        f1 = 2.0 * jnp.exp2(m1 - top)
        f2 = 4.0 * jnp.exp2(m2 - top)
        den = 1.0 / (f0 * s0 + f1 * s1 + f2 * s2)
        w0, w1, w2 = f0 * den, f1 * den, f2 * den
        a2 = wide(a2i[h, 0:DH])
        attended = w0 * a0[h] + w1 * twice(a1[h], 1) + w2 * twice(twice(a2, 1), 1)
        rounded = attended.astype(BF16)
        att[h] = rounded
        attended = wide(rounded)
        rows[h, 0:1, :] = w0
        rows[h, 1:2, :] = w1
        rows[h, 2:3, :] = w2
        squares = jnp.sum(attended * attended, axis=0, keepdims=True)
        dots = jnp.sum(attended * wide(dos[h]), axis=0, keepdims=True)
        rows[h, 3:4, :] = squares
        rows[h, 4:5, :] = dots
        xo[0:1, :] += squares
        xo[1:2, :] += dots

    xo[...] = jnp.zeros_like(xo)
    coarse(0)

    @pl.loop(1, heads)
    def _(h):
        coarse(h)
        combine(h - 1)

    combine(heads - 1)
    x_copy().start()
    x_copy().wait_recv()
    inverse = lax.rsqrt((xo[0:1, :] + xi[0:1, :]) / full_width + EPSILON)
    pull = inverse * inverse * inverse * (xo[1:2, :] + xi[1:2, :]) / full_width

    def cotangents(h):
        w0, w1, w2 = rows[h, 0:1, :], rows[h, 1:2, :], rows[h, 2:3, :]
        grad = inverse * wide(dos[h]) - pull * wide(att[h])
        along = inverse * rows[h, 4:5, :] - pull * rows[h, 3:4, :]
        g2o[h, 0:DH] = fold(fold(w2 * grad)).astype(BF16)
        delta = fold(fold(w2 * along))
        high = wide(delta.astype(BF16))
        g2o[h, DH:PACK] = packed_rows(high, delta - high, delta * 0.0)
        g2_copy(h).start()
        g0[h] = (w0 * grad).astype(BF16)
        g1[h] = fold(w1 * grad).astype(BF16)
        rows[h, 5:6, :] = w0 * along
        rows[h, 6:7, :] = twice(fold(w1 * along), 1)

    each_head(cotangents)

    def score_grads(p, values, grads, delta):
        return (wide(p) * (nn(values, grads) - delta)).astype(BF16)

    def coarse_back(h):
        k1p, v1p = kv1p[h, 0], kv1p[h, 1]
        ds = score_grads(p1[h], v1p, g1[h], rows[h, 6:7, 0:half])
        dk = nn(ds, q1[h])
        dv = nt(p1[h], g1[h])
        dq1[h] = nn(flip(k1p), ds)
        g2_copy(h).wait_recv()
        figures = wide(g2i[h, DH:PACK])
        grads = g2i[h, 0:DH]
        ds = score_grads(p2[h], v2c[h], grads, figures[0:1] + figures[1:2])
        dk2 = nn(ds, q2v[h])
        dv2 = nt(p2[h], grads)
        dq2o[h] = nn(flip(k2c[h]), ds).astype(BF16)
        dq2_copy(h).start()
        dkvo[h, 0] = ((dk + 0.5 * twice(dk2[quarter:], 0)) * SCALE).astype(BF16)
        dkvo[h, 1] = (dv + 0.5 * twice(dv2[quarter:], 0)).astype(BF16)
        dkv_copy(h).start()
        dkv2[h, 0] = dk2[:quarter] * SCALE
        dkv2[h, 1] = dv2[:quarter]

    each_head(coarse_back)

    def level0_back(h):
        outs[0, h] = nt(back[...], (wide(att[h]) * inverse).astype(BF16)).astype(BF16)
        put(0, h).start()
        ds = score_grads(p0[h], vs[h], g0[h], rows[h, 5:6, :])
        dkv0[h, 0] = nn(ds, qs[h]) * SCALE
        dkv0[h, 1] = nt(p0[h], g0[h])
        dq = nn(kts[h], ds) + 0.5 * twice(dq1[h], 1)
        dq2_copy(h).wait_recv()
        dq = (dq + 0.25 * twice(twice(wide(dq2i[h]), 1), 1)) * SCALE
        outs[1, h] = nt(back[...], dq.astype(BF16)).astype(BF16)
        put(1, h).start()

    each_head(level0_back)

    def finish(h):
        dkv_copy(h).wait_recv()
        for n in range(2):
            total = (
                dkv0[h, n] + 0.5 * twice(wide(dkvi[h, n]), 0) + 0.25 * twice(twice(dkv2[h, n], 0), 0)
            )
            outs[2 + n, h] = nn(back[...], total.astype(BF16)).astype(BF16)
            put(2 + n, h).start()

    each_head(finish)

    def drain(h):
        for make in (kv_copy, q2_copy, a2_copy, g2_copy, dkv_copy, dq2_copy):
            make(h).wait_send()
        for n in range(4):
            put(n, h).wait()

    each_head(drain)
    x_copy().wait_send()


def write_out(*refs):
    sources, targets, done = refs[:4], refs[4:8], refs[8]
    rows = sources[0].shape[0] // PIECES
    copies = [
        pltpu.make_async_copy(
            source.at[pl.ds(n * rows, rows)], target.at[pl.ds(n * rows, rows)], done.at[k, n]
        )
        for n in range(PIECES)
        for k, (source, target) in enumerate(zip(sources, targets))
    ]
    for one in copies:
        one.start()
    for one in copies:
        one.wait()


def shards(queries, key_states, value_states, out_grad):
    tokens, width = queries.shape
    heads = width // DH
    half, quarter = tokens // 2, tokens // 4

    def vmem(*shape, dtype=BF16):
        return pltpu.VMEM(shape, dtype)

    scratch = [
        vmem(4, heads, tokens, DH),
        *[vmem(heads, tokens, DH)] * 4,
        vmem(tokens, tokens), vmem(tokens, tokens),
        vmem(heads, tokens, DH), vmem(heads, tokens, DH), vmem(heads, tokens, DH),
        vmem(heads, DH, tokens), vmem(heads, DH, tokens), vmem(heads, DH, tokens),
        vmem(heads, tokens, tokens), vmem(heads, half, half), vmem(heads, half, quarter),
        vmem(heads, DH, tokens, dtype=F32), vmem(heads, DH, half, dtype=F32),
        vmem(heads, 8, tokens, dtype=F32), vmem(heads, DH, tokens),
        vmem(heads, half, DH), vmem(heads, 2, half, DH), vmem(heads, 2, half, DH),
        vmem(heads, half, DH), vmem(heads, half, DH),
        vmem(heads, quarter, DH), vmem(heads, quarter, DH),
        vmem(heads, PACK, quarter), vmem(heads, PACK, quarter),
        vmem(8, tokens, dtype=F32), vmem(8, tokens, dtype=F32),
        vmem(heads, DH, tokens), vmem(heads, DH, half),
        vmem(heads, PACK, quarter), vmem(heads, PACK, quarter),
        vmem(heads, DH, half, dtype=F32),
        vmem(heads, DH, quarter), vmem(heads, DH, quarter),
        vmem(heads, 2, half, DH), vmem(heads, 2, half, DH),
        vmem(heads, 2, tokens, DH, dtype=F32), vmem(heads, 2, quarter, DH, dtype=F32),
        pltpu.SemaphoreType.DMA((7, heads)),
        pltpu.SemaphoreType.DMA((7, heads)),
        pltpu.SemaphoreType.DMA((4, heads)),
        pltpu.SemaphoreType.DMA((4, heads)),
    ]
    flops = 2 * heads * DH * tokens * tokens * 12
    kept = pl.pallas_call(
        kernel,
        out_shape=[jax.ShapeDtypeStruct((tokens, width), BF16)] * 4,
        in_specs=[pl.BlockSpec(memory_space=pltpu.HBM)] * 4,
        out_specs=[pl.BlockSpec(memory_space=pltpu.HBM)] * 4,
        scratch_shapes=scratch,
        compiler_params=pltpu.CompilerParams(
            collective_id=0, has_side_effects=True, vmem_limit_bytes=VMEM
        ),
        cost_estimate=pl.CostEstimate(
            flops=flops, bytes_accessed=16 * tokens * width, transcendentals=heads * tokens * tokens
        ),
        name="hierarchical_attention",
    )(queries, key_states, value_states, out_grad)
    return pl.pallas_call(
        write_out,
        out_shape=[jax.ShapeDtypeStruct((tokens, width), BF16)] * 4,
        in_specs=[pl.BlockSpec(memory_space=pltpu.HBM)] * 4,
        out_specs=[pl.BlockSpec(memory_space=pltpu.HBM)] * 4,
        scratch_shapes=[pltpu.SemaphoreType.DMA((4, PIECES))],
        compiler_params=pltpu.CompilerParams(vmem_limit_bytes=VMEM),
        name="write_out",
    )(*kept)


def solution(mesh):
    return jax.shard_map(
        shards,
        mesh=mesh,
        in_specs=(P("seq", "head"),) * 4,
        out_specs=(P("seq", "head"),) * 4,
        check_vma=False,
    )
```

```python
import functools

import jax
import jax.numpy as jnp
from jax import lax
from jax.experimental import pallas as pl
from jax.experimental.pallas import tpu as pltpu
from jax.sharding import PartitionSpec as P

DH = 128
LEAF = 256
EPSILON = 1e-06
SCALE = DH ** (-0.5)
LOG2 = SCALE * 1.4426950408889634
MESH = pl.DeviceIdType.MESH
F32 = jnp.float32
BF16 = jnp.bfloat16
PIECES = 4
VMEM = 103 * 512 * 1024
PACK = DH + 16


def nn(a, b):
    return lax.dot_general(a, b, (((1,), (0,)), ((), ())), preferred_element_type=F32)


def nt(a, b):
    return lax.dot_general(a, b, (((1,), (1,)), ((), ())), preferred_element_type=F32)


def wide(x):
    return x.astype(F32)


def flip(x):
    return wide(x).T.astype(BF16)


def halve(x):
    half = x.shape[0] // 2
    return ((wide(x[:half]) + wide(x[half:])) * 0.5).astype(BF16)


def twice(x, axis):
    return jnp.concatenate([x, x], axis)


def fold(x):
    half = x.shape[1] // 2
    return x[:, :half] + x[:, half:]


def packed_rows(first, second, third):
    row = lax.broadcasted_iota(jnp.int32, (16, first.shape[1]), 0)
    return jnp.where(row == 0, first, jnp.where(row == 1, second, jnp.where(row == 2, third, 0.0))).astype(BF16)


def kernel(
    q_ref, k_ref, v_ref, g_ref,
    no_ref, gq_ref, gk_ref, gv_ref,
    inq, ink, inv, ing, perm, back, qs, ks, vs, kts, vts, dos, p0, p1, p2, a0, a1, rows, att,
    q1, kv1, kv1p, k2c, v2c, q2, q2v, a2o, a2i, xo, xi,
    g0, g1, g2o, g2i, dq0, dq1, dq2o, dq2i, dkvo, dkvi, dkv0, dkv2,
    send, recv, arrived,
):
    tokens, width = q_ref.shape
    heads = width // DH
    half, quarter = tokens // 2, tokens // 4
    full_width = width * 2
    seq, core = lax.axis_index("seq"), lax.axis_index("head")
    at_x = (seq + 1 - 2 * (seq % 2), core)
    at_y = (seq + 2 - 4 * ((seq // 2) % 2), core)
    at_core = (seq, 1 - core)

    def copy(kind, h, source, target, where):
        return pltpu.make_async_remote_copy(
            src_ref=source, dst_ref=target, send_sem=send.at[kind, h], recv_sem=recv.at[kind, h],
            device_id=where, device_id_type=MESH,
        )

    def kv_copy(h):
        return copy(0, h, kv1.at[h], kv1p.at[h], at_x)

    def q2_copy(h):
        return copy(1, h, q2.at[h], q2v.at[h], at_y)

    def a2_copy(h):
        return copy(2, h, a2o.at[h], a2i.at[h], at_y)

    def g2_copy(h):
        return copy(3, h, g2o.at[h], g2i.at[h], at_y)

    def dkv_copy(h):
        return copy(4, h, dkvo.at[h], dkvi.at[h], at_x)

    def dq2_copy(h):
        return copy(5, h, dq2o.at[h], dq2i.at[h], at_y)

    def x_copy():
        return copy(6, 0, xo, xi, at_core)

    def cols(h):
        return pl.ds(h * DH, DH)

    def each_head(body):
        for h in range(heads):
            body(h)

    def fetch(n, h):
        source, target = ((k_ref, ink), (v_ref, inv), (q_ref, inq), (g_ref, ing))[n]
        return pltpu.make_async_copy(source.at[:, cols(h)], target.at[h], arrived.at[n, h])

    barrier = pltpu.get_barrier_semaphore()
    for where in (at_x, at_y, at_core):
        pl.semaphore_signal(barrier, inc=1, device_id=where, device_id_type=MESH)

    for group in ((0, 1), (2, 3)):
        for h in range(heads):
            for n in group:
                fetch(n, h).start()

    def order(p):
        slab = p // quarter
        return 4 * (p % quarter) + slab // 2 + 2 * (slab % 2)

    shape = (tokens, tokens)
    major = lax.broadcasted_iota(jnp.int32, shape, 0)
    minor = lax.broadcasted_iota(jnp.int32, shape, 1)
    perm[...] = jnp.where(order(major) == minor, 1.0, 0.0).astype(BF16)
    pl.semaphore_wait(barrier, 3)

    def load_kv(h):
        for n, (ref, kept) in enumerate(((ink, ks), (inv, vs))):
            fetch(n, h).wait()
            moved = nn(perm[...], ref[h])
            kept[h] = moved.astype(BF16)
            kv1[h, n] = halve(moved)
        kv_copy(h).start()

    each_head(load_kv)

    def load_q(h):
        fetch(2, h).wait()
        moved = nn(perm[...], inq[h])
        qs[h] = moved.astype(BF16)
        first = halve(moved)
        q1[h] = first
        q2[h] = halve(first)
        q2_copy(h).start()

    each_head(load_q)

    def softmax(scores):
        top = jnp.max(scores, axis=0, keepdims=True)
        e = jnp.exp2((scores - top) * LOG2)
        return top * LOG2, jnp.sum(e, axis=0, keepdims=True), e.astype(BF16)

    def level0(h):
        kts[h] = flip(ks[h])
        vt = flip(vs[h])
        m, s, p = softmax(nt(ks[h], qs[h]))
        p0[h] = p
        a0[h] = nn(vt, p)
        rows[h, 0:1, :] = m
        rows[h, 1:2, :] = s
        dos[h] = nn(perm[...], ing[h]).T.astype(BF16)

    each_head(lambda h: fetch(3, h).wait())
    each_head(level0)
    back[...] = jnp.where(order(minor) == major, 1.0, 0.0).astype(BF16)

    def coarse(h):
        kv_copy(h).wait_recv()
        q2_copy(h).wait_recv()
        k1p, v1p = kv1p[h, 0], kv1p[h, 1]
        k2 = jnp.concatenate([halve(kv1[h, 0]), halve(k1p)], 0)
        v2 = jnp.concatenate([halve(kv1[h, 1]), halve(v1p)], 0)
        k2c[h] = k2
        v2c[h] = v2
        scores = nt(k2, q2v[h]) * LOG2
        m = wide(jnp.max(scores, axis=0, keepdims=True).astype(BF16))
        e = jnp.exp2(scores - m)
        s = jnp.sum(e, axis=0, keepdims=True)
        p = e.astype(BF16)
        p2[h] = p
        a2o[h, 0:DH] = nn(flip(v2), p).astype(BF16)
        high = wide(s.astype(BF16))
        a2o[h, DH:PACK] = packed_rows(m, high, s - high)
        a2_copy(h).start()
        m, s, p = softmax(nt(k1p, q1[h]))
        p1[h] = p
        a1[h] = nn(flip(v1p), p)
        rows[h, 2:3, :] = twice(m, 1)
        rows[h, 3:4, :] = twice(s, 1)

    def combine(h):
        a2_copy(h).wait_recv()
        m0, s0 = rows[h, 0:1, :], rows[h, 1:2, :]
        m1, s1 = rows[h, 2:3, :], rows[h, 3:4, :]
        figures = wide(a2i[h, DH:PACK])
        m2 = twice(twice(figures[0:1], 1), 1)
        s2 = twice(twice(figures[1:2] + figures[2:3], 1), 1)
        top = jnp.maximum(jnp.maximum(m0, m1), m2)
        f0 = jnp.exp2(m0 - top)
        f1 = 2.0 * jnp.exp2(m1 - top)
        f2 = 4.0 * jnp.exp2(m2 - top)
        den = 1.0 / (f0 * s0 + f1 * s1 + f2 * s2)
        w0, w1, w2 = f0 * den, f1 * den, f2 * den
        a2 = wide(a2i[h, 0:DH])
        attended = w0 * a0[h] + w1 * twice(a1[h], 1) + w2 * twice(twice(a2, 1), 1)
        rounded = attended.astype(BF16)
        att[h] = rounded
        attended = wide(rounded)
        rows[h, 0:1, :] = w0
        rows[h, 1:2, :] = w1
        rows[h, 2:3, :] = w2
        squares = jnp.sum(attended * attended, axis=0, keepdims=True)
        dots = jnp.sum(attended * wide(dos[h]), axis=0, keepdims=True)
        rows[h, 3:4, :] = squares
        rows[h, 4:5, :] = dots
        xo[0:1, :] += squares
        xo[1:2, :] += dots

    xo[...] = jnp.zeros_like(xo)
    coarse(0)

    for h in range(1, heads):
        coarse(h)
        combine(h - 1)

    combine(heads - 1)
    x_copy().start()
    x_copy().wait_recv()
    inverse = lax.rsqrt((xo[0:1, :] + xi[0:1, :]) / full_width + EPSILON)
    pull = inverse * inverse * inverse * (xo[1:2, :] + xi[1:2, :]) / full_width

    def cotangents(h):
        w0, w1, w2 = rows[h, 0:1, :], rows[h, 1:2, :], rows[h, 2:3, :]
        grad = inverse * wide(dos[h]) - pull * wide(att[h])
        along = inverse * rows[h, 4:5, :] - pull * rows[h, 3:4, :]
        g2o[h, 0:DH] = fold(fold(w2 * grad)).astype(BF16)
        delta = fold(fold(w2 * along))
        high = wide(delta.astype(BF16))
        g2o[h, DH:PACK] = packed_rows(high, delta - high, delta * 0.0)
        g2_copy(h).start()
        g0[h] = (w0 * grad).astype(BF16)
        g1[h] = fold(w1 * grad).astype(BF16)
        rows[h, 5:6, :] = w0 * along
        rows[h, 6:7, :] = twice(fold(w1 * along), 1)

    each_head(cotangents)

    def score_grads(p, values, grads, delta):
        return (wide(p) * (nn(values, grads) - delta)).astype(BF16)

    def coarse_back(h):
        k1p, v1p = kv1p[h, 0], kv1p[h, 1]
        ds = score_grads(p1[h], v1p, g1[h], rows[h, 6:7, 0:half])
        dk = nn(ds, q1[h])
        dv = nt(p1[h], g1[h])
        dq1[h] = nn(flip(k1p), ds)
        g2_copy(h).wait_recv()
        figures = wide(g2i[h, DH:PACK])
        grads = g2i[h, 0:DH]
        ds = score_grads(p2[h], v2c[h], grads, figures[0:1] + figures[1:2])
        dk2 = nn(ds, q2v[h])
        dv2 = nt(p2[h], grads)
        dq2o[h] = nn(flip(k2c[h]), ds).astype(BF16)
        dq2_copy(h).start()
        dkvo[h, 0] = ((dk + 0.5 * twice(dk2[quarter:], 0)) * SCALE).astype(BF16)
        dkvo[h, 1] = (dv + 0.5 * twice(dv2[quarter:], 0)).astype(BF16)
        dkv_copy(h).start()
        dkv2[h, 0] = dk2[:quarter] * SCALE
        dkv2[h, 1] = dv2[:quarter]

    each_head(coarse_back)

    def level0_back(h):
        no_ref[:, cols(h)] = nt(back[...], (wide(att[h]) * inverse).astype(BF16)).astype(BF16)
        ds = score_grads(p0[h], vs[h], g0[h], rows[h, 5:6, :])
        dkv0[h, 0] = nn(ds, qs[h]) * SCALE
        dkv0[h, 1] = nt(p0[h], g0[h])
        dq0[h] = nn(kts[h], ds) + 0.5 * twice(dq1[h], 1)

    each_head(level0_back)
    each_head(lambda h: dq2_copy(h).wait_recv())

    def finish_q(h):
        dq = dq0[h]
        dq = (dq + 0.25 * twice(twice(wide(dq2i[h]), 1), 1)) * SCALE
        gq_ref[:, cols(h)] = nt(back[...], dq.astype(BF16)).astype(BF16)

    each_head(finish_q)

    def finish(h):
        dkv_copy(h).wait_recv()
        for n, out in enumerate((gk_ref, gv_ref)):
            total = (
                dkv0[h, n] + 0.5 * twice(wide(dkvi[h, n]), 0) + 0.25 * twice(twice(dkv2[h, n], 0), 0)
            )
            out[:, cols(h)] = nn(back[...], total.astype(BF16)).astype(BF16)

    each_head(finish)

    def drain(h):
        for make in (kv_copy, q2_copy, a2_copy, g2_copy, dkv_copy, dq2_copy):
            make(h).wait_send()

    each_head(drain)
    x_copy().wait_send()


def write_out(*refs):
    sources, targets, done = refs[:4], refs[4:8], refs[8]
    rows = sources[0].shape[0] // PIECES
    copies = [
        pltpu.make_async_copy(
            source.at[pl.ds(n * rows, rows)], target.at[pl.ds(n * rows, rows)], done.at[k, n]
        )
        for n in range(PIECES)
        for k, (source, target) in enumerate(zip(sources, targets))
    ]
    for one in copies:
        one.start()
    for one in copies:
        one.wait()


def shards(queries, key_states, value_states, out_grad):
    tokens, width = queries.shape
    heads = width // DH
    half, quarter = tokens // 2, tokens // 4

    def vmem(*shape, dtype=BF16):
        return pltpu.VMEM(shape, dtype)

    scratch = [
        *[vmem(heads, tokens, DH)] * 4,
        vmem(tokens, tokens), vmem(tokens, tokens),
        vmem(heads, tokens, DH), vmem(heads, tokens, DH), vmem(heads, tokens, DH),
        vmem(heads, DH, tokens), vmem(heads, DH, tokens), vmem(heads, DH, tokens),
        vmem(heads, tokens, tokens), vmem(heads, half, half), vmem(heads, half, quarter),
        vmem(heads, DH, tokens, dtype=F32), vmem(heads, DH, half, dtype=F32),
        vmem(heads, 8, tokens, dtype=F32), vmem(heads, DH, tokens),
        vmem(heads, half, DH), vmem(heads, 2, half, DH), vmem(heads, 2, half, DH),
        vmem(heads, half, DH), vmem(heads, half, DH),
        vmem(heads, quarter, DH), vmem(heads, quarter, DH),
        vmem(heads, PACK, quarter), vmem(heads, PACK, quarter),
        vmem(8, tokens, dtype=F32), vmem(8, tokens, dtype=F32),
        vmem(heads, DH, tokens), vmem(heads, DH, half),
        vmem(heads, PACK, quarter), vmem(heads, PACK, quarter),
        vmem(heads, DH, tokens, dtype=F32), vmem(heads, DH, half, dtype=F32),
        vmem(heads, DH, quarter), vmem(heads, DH, quarter),
        vmem(heads, 2, half, DH), vmem(heads, 2, half, DH),
        vmem(heads, 2, tokens, DH, dtype=F32), vmem(heads, 2, quarter, DH, dtype=F32),
        pltpu.SemaphoreType.DMA((7, heads)),
        pltpu.SemaphoreType.DMA((7, heads)),
        pltpu.SemaphoreType.DMA((4, heads)),
    ]
    flops = 2 * heads * DH * tokens * tokens * 12
    kept = pl.pallas_call(
        kernel,
        out_shape=[jax.ShapeDtypeStruct((tokens, width), BF16)] * 4,
        in_specs=[pl.BlockSpec(memory_space=pltpu.HBM)] * 4,
        out_specs=[pl.BlockSpec(memory_space=pltpu.VMEM)] * 4,
        scratch_shapes=scratch,
        compiler_params=pltpu.CompilerParams(
            collective_id=0, has_side_effects=True, vmem_limit_bytes=VMEM
        ),
        cost_estimate=pl.CostEstimate(
            flops=flops, bytes_accessed=16 * tokens * width, transcendentals=heads * tokens * tokens
        ),
        name="hierarchical_attention",
    )(queries, key_states, value_states, out_grad)
    return pl.pallas_call(
        write_out,
        out_shape=[jax.ShapeDtypeStruct((tokens, width), BF16)] * 4,
        in_specs=[pl.BlockSpec(memory_space=pltpu.VMEM)] * 4,
        out_specs=[pl.BlockSpec(memory_space=pltpu.HBM)] * 4,
        scratch_shapes=[pltpu.SemaphoreType.DMA((4, PIECES))],
        compiler_params=pltpu.CompilerParams(vmem_limit_bytes=VMEM),
        name="write_out",
    )(*kept)


def solution(mesh):
    return jax.shard_map(
        shards,
        mesh=mesh,
        in_specs=(P("seq", "head"),) * 4,
        out_specs=(P("seq", "head"),) * 4,
        check_vma=False,
    )
```

```python
import functools

import jax
import jax.numpy as jnp
from jax import lax
from jax.experimental import pallas as pl
from jax.experimental.pallas import tpu as pltpu
from jax.sharding import PartitionSpec as P

DH = 128
LEAF = 256
EPSILON = 1e-06
SCALE = DH ** (-0.5)
LOG2 = SCALE * 1.4426950408889634
MESH = pl.DeviceIdType.MESH
F32 = jnp.float32
BF16 = jnp.bfloat16
PIECES = 4
VMEM = 103 * 512 * 1024
PACK = DH + 16


def nn(a, b):
    return lax.dot_general(a, b, (((1,), (0,)), ((), ())), preferred_element_type=F32)


def nt(a, b):
    return lax.dot_general(a, b, (((1,), (1,)), ((), ())), preferred_element_type=F32)


def wide(x):
    return x.astype(F32)


def flip(x):
    return wide(x).T.astype(BF16)


def halve(x):
    half = x.shape[0] // 2
    return ((wide(x[:half]) + wide(x[half:])) * 0.5).astype(BF16)


def twice(x, axis):
    return jnp.concatenate([x, x], axis)


def fold(x):
    half = x.shape[1] // 2
    return x[:, :half] + x[:, half:]


def packed_rows(first, second, third):
    row = lax.broadcasted_iota(jnp.int32, (16, first.shape[1]), 0)
    return jnp.where(row == 0, first, jnp.where(row == 1, second, jnp.where(row == 2, third, 0.0))).astype(BF16)


def kernel(
    q_ref, k_ref, v_ref, g_ref,
    no_ref, gq_ref, gk_ref, gv_ref,
    inq, ink, inv, ing, perm, back, qs, ks, vs, kts, vts, dos, p0, p1, p2, a0, a1, rows, att,
    q1, kv1, kv1p, k2c, v2c, q2, q2v, a2o, a2i, xo, xi,
    g0, g1, g2o, g2i, dq0, dq1, dq2o, dq2i, dkvo, dkvi, dkv0, dkv1, dkv2,
    send, recv, arrived,
):
    tokens, width = q_ref.shape
    heads = width // DH
    half, quarter = tokens // 2, tokens // 4
    full_width = width * 2
    seq, core = lax.axis_index("seq"), lax.axis_index("head")
    at_x = (seq + 1 - 2 * (seq % 2), core)
    at_y = (seq + 2 - 4 * ((seq // 2) % 2), core)
    at_core = (seq, 1 - core)

    def copy(kind, h, source, target, where):
        return pltpu.make_async_remote_copy(
            src_ref=source, dst_ref=target, send_sem=send.at[kind, h], recv_sem=recv.at[kind, h],
            device_id=where, device_id_type=MESH,
        )

    def kv_copy(h):
        return copy(0, h, kv1.at[h], kv1p.at[h], at_x)

    def q2_copy(h):
        return copy(1, h, q2.at[h], q2v.at[h], at_y)

    def a2_copy(h):
        return copy(2, h, a2o.at[h], a2i.at[h], at_y)

    def g2_copy(h):
        return copy(3, h, g2o.at[h], g2i.at[h], at_y)

    def dkv_copy(h):
        return copy(4, h, dkvo.at[h], dkvi.at[h], at_x)

    def dq2_copy(h):
        return copy(5, h, dq2o.at[h], dq2i.at[h], at_y)

    def x_copy():
        return copy(6, 0, xo, xi, at_core)

    def cols(h):
        return pl.ds(h * DH, DH)

    def each_head(body):
        for h in range(heads):
            body(h)

    def fetch(n, h):
        source, target = ((k_ref, ink), (v_ref, inv), (q_ref, inq), (g_ref, ing))[n]
        return pltpu.make_async_copy(source.at[:, cols(h)], target.at[h], arrived.at[n, h])

    barrier = pltpu.get_barrier_semaphore()
    for where in (at_x, at_y, at_core):
        pl.semaphore_signal(barrier, inc=1, device_id=where, device_id_type=MESH)

    for group in ((0, 1), (2, 3)):
        for h in range(heads):
            for n in group:
                fetch(n, h).start()

    bits = quarter.bit_length() - 1
    lane = lax.broadcasted_iota(jnp.int32, (1, tokens), 1)
    slab = lane >> bits
    token_of = ((lane & (quarter - 1)) << 2) + (slab >> 1) + ((slab & 1) << 1)
    place_of = (lane >> 2) + (((lane >> 1) & 1) << bits) + ((lane & 1) << (bits + 1))
    major = lax.broadcasted_iota(jnp.int32, (tokens, tokens), 0)
    perm[...] = jnp.where(place_of == major, 1.0, 0.0).astype(BF16)
    pl.semaphore_wait(barrier, 3)

    def load_kv(h):
        for n, (ref, kept) in enumerate(((ink, ks), (inv, vs))):
            fetch(n, h).wait()
            moved = nn(perm[...], ref[h])
            kept[h] = moved.astype(BF16)
            kv1[h, n] = halve(moved)
        kv_copy(h).start()

    each_head(load_kv)

    def load_q(h):
        fetch(2, h).wait()
        moved = nn(perm[...], inq[h])
        qs[h] = moved.astype(BF16)
        first = halve(moved)
        q1[h] = first
        q2[h] = halve(first)
        q2_copy(h).start()

    each_head(load_q)

    def softmax(scores):
        top = jnp.max(scores, axis=0, keepdims=True)
        e = jnp.exp2((scores - top) * LOG2)
        return top * LOG2, jnp.sum(e, axis=0, keepdims=True), e.astype(BF16)

    def level0(h):
        kts[h] = flip(ks[h])
        vt = flip(vs[h])
        m, s, p = softmax(nt(ks[h], qs[h]))
        p0[h] = p
        a0[h] = nn(vt, p)
        rows[h, 0:1, :] = m
        rows[h, 1:2, :] = s
        dos[h] = nn(perm[...], ing[h]).T.astype(BF16)

    each_head(lambda h: fetch(3, h).wait())
    each_head(level0)
    back[...] = jnp.where(token_of == major, 1.0, 0.0).astype(BF16)

    def coarse(h):
        kv_copy(h).wait_recv()
        q2_copy(h).wait_recv()
        k1p, v1p = kv1p[h, 0], kv1p[h, 1]
        k2 = jnp.concatenate([halve(kv1[h, 0]), halve(k1p)], 0)
        v2 = jnp.concatenate([halve(kv1[h, 1]), halve(v1p)], 0)
        k2c[h] = k2
        v2c[h] = v2
        scores = nt(k2, q2v[h]) * LOG2
        m = wide(jnp.max(scores, axis=0, keepdims=True).astype(BF16))
        e = jnp.exp2(scores - m)
        s = jnp.sum(e, axis=0, keepdims=True)
        p = e.astype(BF16)
        p2[h] = p
        a2o[h, 0:DH] = nn(flip(v2), p).astype(BF16)
        high = wide(s.astype(BF16))
        a2o[h, DH:PACK] = packed_rows(m, high, s - high)
        a2_copy(h).start()
        m, s, p = softmax(nt(k1p, q1[h]))
        p1[h] = p
        a1[h] = nn(flip(v1p), p)
        rows[h, 2:3, :] = twice(m, 1)
        rows[h, 3:4, :] = twice(s, 1)

    def combine(h):
        a2_copy(h).wait_recv()
        m0, s0 = rows[h, 0:1, :], rows[h, 1:2, :]
        m1, s1 = rows[h, 2:3, :], rows[h, 3:4, :]
        figures = wide(a2i[h, DH:PACK])
        m2 = twice(twice(figures[0:1], 1), 1)
        s2 = twice(twice(figures[1:2] + figures[2:3], 1), 1)
        top = jnp.maximum(jnp.maximum(m0, m1), m2)
        f0 = jnp.exp2(m0 - top)
        f1 = 2.0 * jnp.exp2(m1 - top)
        f2 = 4.0 * jnp.exp2(m2 - top)
        den = 1.0 / (f0 * s0 + f1 * s1 + f2 * s2)
        w0, w1, w2 = f0 * den, f1 * den, f2 * den
        a2 = wide(a2i[h, 0:DH])
        attended = w0 * a0[h] + w1 * twice(a1[h], 1) + w2 * twice(twice(a2, 1), 1)
        rounded = attended.astype(BF16)
        att[h] = rounded
        attended = wide(rounded)
        rows[h, 0:1, :] = w0
        rows[h, 1:2, :] = w1
        rows[h, 2:3, :] = w2
        squares = jnp.sum(attended * attended, axis=0, keepdims=True)
        dots = jnp.sum(attended * wide(dos[h]), axis=0, keepdims=True)
        rows[h, 3:4, :] = squares
        rows[h, 4:5, :] = dots
        xo[0:1, :] += squares
        xo[1:2, :] += dots

    xo[...] = jnp.zeros_like(xo)
    coarse(0)

    for h in range(1, heads):
        coarse(h)
        combine(h - 1)

    combine(heads - 1)
    x_copy().start()
    x_copy().wait_recv()
    inverse = lax.rsqrt((xo[0:1, :] + xi[0:1, :]) / full_width + EPSILON)
    pull = inverse * inverse * inverse * (xo[1:2, :] + xi[1:2, :]) / full_width

    def cotangents(h):
        w0, w1, w2 = rows[h, 0:1, :], rows[h, 1:2, :], rows[h, 2:3, :]
        grad = inverse * wide(dos[h]) - pull * wide(att[h])
        along = inverse * rows[h, 4:5, :] - pull * rows[h, 3:4, :]
        g2o[h, 0:DH] = fold(fold(w2 * grad)).astype(BF16)
        delta = fold(fold(w2 * along))
        high = wide(delta.astype(BF16))
        g2o[h, DH:PACK] = packed_rows(high, delta - high, delta * 0.0)
        g2_copy(h).start()
        g0[h] = (w0 * grad).astype(BF16)
        g1[h] = fold(w1 * grad).astype(BF16)
        rows[h, 5:6, :] = w0 * along
        rows[h, 6:7, :] = twice(fold(w1 * along), 1)

    def score_grads(p, values, grads, delta):
        return (wide(p) * (nn(values, grads) - delta)).astype(BF16)

    def level1_back(h):
        k1p, v1p = kv1p[h, 0], kv1p[h, 1]
        ds = score_grads(p1[h], v1p, g1[h], rows[h, 6:7, 0:half])
        dkv1[0] = nn(ds, q1[h])
        dkv1[1] = nt(p1[h], g1[h])
        dq1[h] = nn(flip(k1p), ds)

    def level2_back(h):
        g2_copy(h).wait_recv()
        figures = wide(g2i[h, DH:PACK])
        grads = g2i[h, 0:DH]
        ds = score_grads(p2[h], v2c[h], grads, figures[0:1] + figures[1:2])
        dk2 = nn(ds, q2v[h])
        dv2 = nt(p2[h], grads)
        dq2o[h] = nn(flip(k2c[h]), ds).astype(BF16)
        dq2_copy(h).start()
        dkvo[h, 0] = ((dkv1[0] + 0.5 * twice(dk2[quarter:], 0)) * SCALE).astype(BF16)
        dkvo[h, 1] = (dkv1[1] + 0.5 * twice(dv2[quarter:], 0)).astype(BF16)
        dkv_copy(h).start()
        dkv2[h, 0] = dk2[:quarter] * SCALE
        dkv2[h, 1] = dv2[:quarter]

    cotangents(0)
    cotangents(1)
    level1_back(0)
    for h in range(2, heads):
        cotangents(h)
    level2_back(0)
    for h in range(1, heads):
        level1_back(h)
        level2_back(h)

    def level0_back(h):
        no_ref[:, cols(h)] = nt(back[...], (wide(att[h]) * inverse).astype(BF16)).astype(BF16)
        ds = score_grads(p0[h], vs[h], g0[h], rows[h, 5:6, :])
        dkv0[h, 0] = nn(ds, qs[h]) * SCALE
        dkv0[h, 1] = nt(p0[h], g0[h])
        dq0[h] = nn(kts[h], ds) + 0.5 * twice(dq1[h], 1)

    each_head(level0_back)
    each_head(lambda h: dq2_copy(h).wait_recv())

    def finish_q(h):
        dq = dq0[h]
        dq = (dq + 0.25 * twice(twice(wide(dq2i[h]), 1), 1)) * SCALE
        gq_ref[:, cols(h)] = nt(back[...], dq.astype(BF16)).astype(BF16)

    each_head(finish_q)

    def finish(h):
        dkv_copy(h).wait_recv()
        for n, out in enumerate((gk_ref, gv_ref)):
            total = (
                dkv0[h, n] + 0.5 * twice(wide(dkvi[h, n]), 0) + 0.25 * twice(twice(dkv2[h, n], 0), 0)
            )
            out[:, cols(h)] = nn(back[...], total.astype(BF16)).astype(BF16)

    each_head(finish)

    def drain(h):
        for make in (kv_copy, q2_copy, a2_copy, g2_copy, dkv_copy, dq2_copy):
            make(h).wait_send()

    each_head(drain)
    x_copy().wait_send()


def write_out(*refs):
    sources, targets, done = refs[:4], refs[4:8], refs[8]
    rows = sources[0].shape[0] // PIECES
    copies = [
        pltpu.make_async_copy(
            source.at[pl.ds(n * rows, rows)], target.at[pl.ds(n * rows, rows)], done.at[k, n]
        )
        for n in range(PIECES)
        for k, (source, target) in enumerate(zip(sources, targets))
    ]
    for one in copies:
        one.start()
    for one in copies:
        one.wait()


def shards(queries, key_states, value_states, out_grad):
    tokens, width = queries.shape
    heads = width // DH
    half, quarter = tokens // 2, tokens // 4

    def vmem(*shape, dtype=BF16):
        return pltpu.VMEM(shape, dtype)

    scratch = [
        *[vmem(heads, tokens, DH)] * 4,
        vmem(tokens, tokens), vmem(tokens, tokens),
        vmem(heads, tokens, DH), vmem(heads, tokens, DH), vmem(heads, tokens, DH),
        vmem(heads, DH, tokens), vmem(heads, DH, tokens), vmem(heads, DH, tokens),
        vmem(heads, tokens, tokens), vmem(heads, half, half), vmem(heads, half, quarter),
        vmem(heads, DH, tokens, dtype=F32), vmem(heads, DH, half, dtype=F32),
        vmem(heads, 8, tokens, dtype=F32), vmem(heads, DH, tokens),
        vmem(heads, half, DH), vmem(heads, 2, half, DH), vmem(heads, 2, half, DH),
        vmem(heads, half, DH), vmem(heads, half, DH),
        vmem(heads, quarter, DH), vmem(heads, quarter, DH),
        vmem(heads, PACK, quarter), vmem(heads, PACK, quarter),
        vmem(8, tokens, dtype=F32), vmem(8, tokens, dtype=F32),
        vmem(heads, DH, tokens), vmem(heads, DH, half),
        vmem(heads, PACK, quarter), vmem(heads, PACK, quarter),
        vmem(heads, DH, tokens, dtype=F32), vmem(heads, DH, half, dtype=F32),
        vmem(heads, DH, quarter), vmem(heads, DH, quarter),
        vmem(heads, 2, half, DH), vmem(heads, 2, half, DH),
        vmem(heads, 2, tokens, DH, dtype=F32), vmem(2, half, DH, dtype=F32),
        vmem(heads, 2, quarter, DH, dtype=F32),
        pltpu.SemaphoreType.DMA((7, heads)),
        pltpu.SemaphoreType.DMA((7, heads)),
        pltpu.SemaphoreType.DMA((4, heads)),
    ]
    flops = 2 * heads * DH * tokens * tokens * 12
    kept = pl.pallas_call(
        kernel,
        out_shape=[jax.ShapeDtypeStruct((tokens, width), BF16)] * 4,
        in_specs=[pl.BlockSpec(memory_space=pltpu.HBM)] * 4,
        out_specs=[pl.BlockSpec(memory_space=pltpu.VMEM)] * 4,
        scratch_shapes=scratch,
        compiler_params=pltpu.CompilerParams(
            collective_id=0, has_side_effects=True, vmem_limit_bytes=VMEM
        ),
        cost_estimate=pl.CostEstimate(
            flops=flops, bytes_accessed=16 * tokens * width, transcendentals=heads * tokens * tokens
        ),
        name="hierarchical_attention",
    )(queries, key_states, value_states, out_grad)
    return pl.pallas_call(
        write_out,
        out_shape=[jax.ShapeDtypeStruct((tokens, width), BF16)] * 4,
        in_specs=[pl.BlockSpec(memory_space=pltpu.VMEM)] * 4,
        out_specs=[pl.BlockSpec(memory_space=pltpu.HBM)] * 4,
        scratch_shapes=[pltpu.SemaphoreType.DMA((4, PIECES))],
        compiler_params=pltpu.CompilerParams(vmem_limit_bytes=VMEM),
        name="write_out",
    )(*kept)


def solution(mesh):
    return jax.shard_map(
        shards,
        mesh=mesh,
        in_specs=(P("seq", "head"),) * 4,
        out_specs=(P("seq", "head"),) * 4,
        check_vma=False,
    )
```

```python
import functools

import jax
import jax.numpy as jnp
from jax import lax
from jax.experimental import pallas as pl
from jax.experimental.pallas import tpu as pltpu
from jax.sharding import PartitionSpec as P

DH = 128
LEAF = 256
EPSILON = 1e-06
SCALE = DH ** (-0.5)
LOG2 = SCALE * 1.4426950408889634
MESH = pl.DeviceIdType.MESH
F32 = jnp.float32
BF16 = jnp.bfloat16
PIECES = 4
VMEM = 103 * 512 * 1024
PACK = DH + 16


def nn(a, b):
    return lax.dot_general(a, b, (((1,), (0,)), ((), ())), preferred_element_type=F32)


def nt(a, b):
    return lax.dot_general(a, b, (((1,), (1,)), ((), ())), preferred_element_type=F32)


def wide(x):
    return x.astype(F32)


def flip(x):
    return wide(x).T.astype(BF16)


def halve(x):
    half = x.shape[0] // 2
    return ((wide(x[:half]) + wide(x[half:])) * 0.5).astype(BF16)


def twice(x, axis):
    return jnp.concatenate([x, x], axis)


def fold(x):
    half = x.shape[1] // 2
    return x[:, :half] + x[:, half:]


def packed_rows(first, second, third):
    row = lax.broadcasted_iota(jnp.int32, (16, first.shape[1]), 0)
    return jnp.where(row == 0, first, jnp.where(row == 1, second, jnp.where(row == 2, third, 0.0))).astype(BF16)


def kernel(
    q_ref, k_ref, v_ref, g_ref,
    no_ref, gq_ref, gk_ref, gv_ref,
    inkv, inqg, perm, back, qs, ks, vs, kts, vts, dos, p0, p1, p2, a0, a1, rows, att,
    q1, kv1, kv1p, k2c, v2c, q2, q2v, a2o, a2i, xo, xi,
    g0, g1, g2o, g2i, dq0, dq1, dq2o, dq2i, dkvo, dkvi, dkv0, dkv1, dkv2,
    send, recv, arrived,
):
    tokens, width = q_ref.shape
    heads = width // DH
    half, quarter = tokens // 2, tokens // 4
    full_width = width * 2
    seq, core = lax.axis_index("seq"), lax.axis_index("head")
    at_x = (seq + 1 - 2 * (seq % 2), core)
    at_y = (seq + 2 - 4 * ((seq // 2) % 2), core)
    at_core = (seq, 1 - core)

    def copy(kind, h, source, target, where):
        return pltpu.make_async_remote_copy(
            src_ref=source, dst_ref=target, send_sem=send.at[kind, h], recv_sem=recv.at[kind, h],
            device_id=where, device_id_type=MESH,
        )

    def kv_copy(h):
        return copy(0, h, kv1.at[h], kv1p.at[h], at_x)

    def q2_copy(h):
        return copy(1, h, q2.at[h], q2v.at[h], at_y)

    def a2_copy(h):
        return copy(2, h, a2o.at[h], a2i.at[h], at_y)

    def g2_copy(h):
        return copy(3, h, g2o.at[h], g2i.at[h], at_y)

    def dkv_copy(h):
        return copy(4, h, dkvo.at[h], dkvi.at[h], at_x)

    def dq2_copy(h):
        return copy(5, h, dq2o.at[h], dq2i.at[h], at_y)

    def x_copy():
        return copy(6, 0, xo, xi, at_core)

    def cols(h):
        return pl.ds(h * DH, DH)

    def each_head(body):
        for h in range(heads):
            body(h)

    def fetch(n, h):
        source, target = ((k_ref, inkv), (v_ref, inkv), (q_ref, inqg), (g_ref, inqg))[n]
        return pltpu.make_async_copy(
            source.at[:, cols(h)], target.at[h, :, cols(n % 2)], arrived.at[n, h]
        )

    barrier = pltpu.get_barrier_semaphore()
    for where in (at_x, at_y, at_core):
        pl.semaphore_signal(barrier, inc=1, device_id=where, device_id_type=MESH)

    for h in range(heads):
        for n in range(4):
            fetch(n, h).start()

    bits = quarter.bit_length() - 1
    lane = lax.broadcasted_iota(jnp.int32, (1, tokens), 1)
    slab = lane >> bits
    token_of = ((lane & (quarter - 1)) << 2) + (slab >> 1) + ((slab & 1) << 1)
    place_of = (lane >> 2) + (((lane >> 1) & 1) << bits) + ((lane & 1) << (bits + 1))
    major = lax.broadcasted_iota(jnp.int32, (tokens, tokens), 0)
    perm[...] = jnp.where(place_of == major, 1.0, 0.0).astype(BF16)
    pl.semaphore_wait(barrier, 3)

    def load(h):
        fetch(0, h).wait()
        fetch(1, h).wait()
        moved = nn(perm[...], inkv[h])
        for n, kept in enumerate((ks, vs)):
            kept[h] = moved[:, n * DH : (n + 1) * DH].astype(BF16)
            kv1[h, n] = halve(moved[:, n * DH : (n + 1) * DH])
        kv_copy(h).start()
        fetch(2, h).wait()
        fetch(3, h).wait()
        moved = nn(perm[...], inqg[h])
        qs[h] = moved[:, :DH].astype(BF16)
        first = halve(moved[:, :DH])
        q1[h] = first
        q2[h] = halve(first)
        q2_copy(h).start()
        dos[h] = moved[:, DH:].T.astype(BF16)

    each_head(load)

    def softmax(scores):
        top = jnp.max(scores, axis=0, keepdims=True)
        e = jnp.exp2((scores - top) * LOG2)
        return top * LOG2, jnp.sum(e, axis=0, keepdims=True), e.astype(BF16)

    def level0(h):
        kts[h] = flip(ks[h])
        vt = flip(vs[h])
        m, s, p = softmax(nt(ks[h], qs[h]))
        p0[h] = p
        a0[h] = nn(vt, p)
        rows[h, 0:1, :] = m
        rows[h, 1:2, :] = s

    each_head(level0)
    back[...] = jnp.where(token_of == major, 1.0, 0.0).astype(BF16)

    def coarse(h):
        kv_copy(h).wait_recv()
        q2_copy(h).wait_recv()
        k1p, v1p = kv1p[h, 0], kv1p[h, 1]
        k2 = jnp.concatenate([halve(kv1[h, 0]), halve(k1p)], 0)
        v2 = jnp.concatenate([halve(kv1[h, 1]), halve(v1p)], 0)
        k2c[h] = k2
        v2c[h] = v2
        scores = nt(k2, q2v[h]) * LOG2
        m = wide(jnp.max(scores, axis=0, keepdims=True).astype(BF16))
        e = jnp.exp2(scores - m)
        s = jnp.sum(e, axis=0, keepdims=True)
        p = e.astype(BF16)
        p2[h] = p
        a2o[h, 0:DH] = nn(flip(v2), p).astype(BF16)
        high = wide(s.astype(BF16))
        a2o[h, DH:PACK] = packed_rows(m, high, s - high)
        a2_copy(h).start()
        m, s, p = softmax(nt(k1p, q1[h]))
        p1[h] = p
        a1[h] = nn(flip(v1p), p)
        rows[h, 2:3, :] = twice(m, 1)
        rows[h, 3:4, :] = twice(s, 1)

    def combine(h):
        a2_copy(h).wait_recv()
        m0, s0 = rows[h, 0:1, :], rows[h, 1:2, :]
        m1, s1 = rows[h, 2:3, :], rows[h, 3:4, :]
        figures = wide(a2i[h, DH:PACK])
        m2 = twice(twice(figures[0:1], 1), 1)
        s2 = twice(twice(figures[1:2] + figures[2:3], 1), 1)
        top = jnp.maximum(jnp.maximum(m0, m1), m2)
        f0 = jnp.exp2(m0 - top)
        f1 = 2.0 * jnp.exp2(m1 - top)
        f2 = 4.0 * jnp.exp2(m2 - top)
        den = 1.0 / (f0 * s0 + f1 * s1 + f2 * s2)
        w0, w1, w2 = f0 * den, f1 * den, f2 * den
        a2 = wide(a2i[h, 0:DH])
        attended = w0 * a0[h] + w1 * twice(a1[h], 1) + w2 * twice(twice(a2, 1), 1)
        rounded = attended.astype(BF16)
        att[h] = rounded
        attended = wide(rounded)
        rows[h, 0:1, :] = w0
        rows[h, 1:2, :] = w1
        rows[h, 2:3, :] = w2
        squares = jnp.sum(attended * attended, axis=0, keepdims=True)
        dots = jnp.sum(attended * wide(dos[h]), axis=0, keepdims=True)
        rows[h, 3:4, :] = squares
        rows[h, 4:5, :] = dots
        xo[0:1, :] += squares
        xo[1:2, :] += dots

    xo[...] = jnp.zeros_like(xo)
    coarse(0)

    for h in range(1, heads):
        coarse(h)
        combine(h - 1)

    combine(heads - 1)
    x_copy().start()
    x_copy().wait_recv()
    inverse = lax.rsqrt((xo[0:1, :] + xi[0:1, :]) / full_width + EPSILON)
    pull = inverse * inverse * inverse * (xo[1:2, :] + xi[1:2, :]) / full_width

    def cotangents(h):
        w0, w1, w2 = rows[h, 0:1, :], rows[h, 1:2, :], rows[h, 2:3, :]
        grad = inverse * wide(dos[h]) - pull * wide(att[h])
        along = inverse * rows[h, 4:5, :] - pull * rows[h, 3:4, :]
        g2o[h, 0:DH] = fold(fold(w2 * grad)).astype(BF16)
        delta = fold(fold(w2 * along))
        high = wide(delta.astype(BF16))
        g2o[h, DH:PACK] = packed_rows(high, delta - high, delta * 0.0)
        g2_copy(h).start()
        g0[h] = (w0 * grad).astype(BF16)
        g1[h] = fold(w1 * grad).astype(BF16)
        rows[h, 5:6, :] = w0 * along
        rows[h, 6:7, :] = twice(fold(w1 * along), 1)

    def score_grads(p, values, grads, delta):
        return (wide(p) * (nn(values, grads) - delta)).astype(BF16)

    def level1_back(h):
        k1p, v1p = kv1p[h, 0], kv1p[h, 1]
        ds = score_grads(p1[h], v1p, g1[h], rows[h, 6:7, 0:half])
        dkv1[0] = nn(ds, q1[h])
        dkv1[1] = nt(p1[h], g1[h])
        dq1[h] = nn(flip(k1p), ds)

    def level2_back(h):
        g2_copy(h).wait_recv()
        figures = wide(g2i[h, DH:PACK])
        grads = g2i[h, 0:DH]
        ds = score_grads(p2[h], v2c[h], grads, figures[0:1] + figures[1:2])
        dk2 = nn(ds, q2v[h])
        dv2 = nt(p2[h], grads)
        dq2o[h] = nn(flip(k2c[h]), ds).astype(BF16)
        dq2_copy(h).start()
        dkvo[h, 0] = ((dkv1[0] + 0.5 * twice(dk2[quarter:], 0)) * SCALE).astype(BF16)
        dkvo[h, 1] = (dkv1[1] + 0.5 * twice(dv2[quarter:], 0)).astype(BF16)
        dkv_copy(h).start()
        dkv2[h, 0] = dk2[:quarter] * SCALE
        dkv2[h, 1] = dv2[:quarter]

    cotangents(0)
    cotangents(1)
    level1_back(0)
    for h in range(2, heads):
        cotangents(h)
    level2_back(0)
    for h in range(1, heads):
        level1_back(h)
        level2_back(h)

    def level0_back(h):
        ds = score_grads(p0[h], vs[h], g0[h], rows[h, 5:6, :])
        dkv0[h, 0] = nn(ds, qs[h]) * SCALE
        dkv0[h, 1] = nt(p0[h], g0[h])
        dq0[h] = nn(kts[h], ds) + 0.5 * twice(dq1[h], 1)

    each_head(level0_back)
    each_head(lambda h: dq2_copy(h).wait_recv())

    def finish_q(h):
        dq = dq0[h]
        dq = (dq + 0.25 * twice(twice(wide(dq2i[h]), 1), 1)) * SCALE
        pair = jnp.concatenate([(wide(att[h]) * inverse).astype(BF16), dq.astype(BF16)], 0)
        ordered = nt(back[...], pair).astype(BF16)
        no_ref[:, cols(h)] = ordered[:, :DH]
        gq_ref[:, cols(h)] = ordered[:, DH:]

    each_head(finish_q)

    def finish(h):
        dkv_copy(h).wait_recv()
        pair = jnp.concatenate(
            [
                dkv0[h, n] + 0.5 * twice(wide(dkvi[h, n]), 0) + 0.25 * twice(twice(dkv2[h, n], 0), 0)
                for n in range(2)
            ],
            1,
        )
        ordered = nn(back[...], pair.astype(BF16)).astype(BF16)
        gk_ref[:, cols(h)] = ordered[:, :DH]
        gv_ref[:, cols(h)] = ordered[:, DH:]

    each_head(finish)

    def drain(h):
        for make in (kv_copy, q2_copy, a2_copy, g2_copy, dkv_copy, dq2_copy):
            make(h).wait_send()

    each_head(drain)
    x_copy().wait_send()


def write_out(*refs):
    sources, targets, done = refs[:4], refs[4:8], refs[8]
    rows = sources[0].shape[0] // PIECES
    copies = [
        pltpu.make_async_copy(
            source.at[pl.ds(n * rows, rows)], target.at[pl.ds(n * rows, rows)], done.at[k, n]
        )
        for n in range(PIECES)
        for k, (source, target) in enumerate(zip(sources, targets))
    ]
    for one in copies:
        one.start()
    for one in copies:
        one.wait()


def shards(queries, key_states, value_states, out_grad):
    tokens, width = queries.shape
    heads = width // DH
    half, quarter = tokens // 2, tokens // 4

    def vmem(*shape, dtype=BF16):
        return pltpu.VMEM(shape, dtype)

    scratch = [
        vmem(heads, tokens, 2 * DH), vmem(heads, tokens, 2 * DH),
        vmem(tokens, tokens), vmem(tokens, tokens),
        vmem(heads, tokens, DH), vmem(heads, tokens, DH), vmem(heads, tokens, DH),
        vmem(heads, DH, tokens), vmem(heads, DH, tokens), vmem(heads, DH, tokens),
        vmem(heads, tokens, tokens), vmem(heads, half, half), vmem(heads, half, quarter),
        vmem(heads, DH, tokens, dtype=F32), vmem(heads, DH, half, dtype=F32),
        vmem(heads, 8, tokens, dtype=F32), vmem(heads, DH, tokens),
        vmem(heads, half, DH), vmem(heads, 2, half, DH), vmem(heads, 2, half, DH),
        vmem(heads, half, DH), vmem(heads, half, DH),
        vmem(heads, quarter, DH), vmem(heads, quarter, DH),
        vmem(heads, PACK, quarter), vmem(heads, PACK, quarter),
        vmem(8, tokens, dtype=F32), vmem(8, tokens, dtype=F32),
        vmem(heads, DH, tokens), vmem(heads, DH, half),
        vmem(heads, PACK, quarter), vmem(heads, PACK, quarter),
        vmem(heads, DH, tokens, dtype=F32), vmem(heads, DH, half, dtype=F32),
        vmem(heads, DH, quarter), vmem(heads, DH, quarter),
        vmem(heads, 2, half, DH), vmem(heads, 2, half, DH),
        vmem(heads, 2, tokens, DH, dtype=F32), vmem(2, half, DH, dtype=F32),
        vmem(heads, 2, quarter, DH, dtype=F32),
        pltpu.SemaphoreType.DMA((7, heads)),
        pltpu.SemaphoreType.DMA((7, heads)),
        pltpu.SemaphoreType.DMA((4, heads)),
    ]
    flops = 2 * heads * DH * tokens * tokens * 12
    kept = pl.pallas_call(
        kernel,
        out_shape=[jax.ShapeDtypeStruct((tokens, width), BF16)] * 4,
        in_specs=[pl.BlockSpec(memory_space=pltpu.HBM)] * 4,
        out_specs=[pl.BlockSpec(memory_space=pltpu.VMEM)] * 4,
        scratch_shapes=scratch,
        compiler_params=pltpu.CompilerParams(
            collective_id=0, has_side_effects=True, vmem_limit_bytes=VMEM
        ),
        cost_estimate=pl.CostEstimate(
            flops=flops, bytes_accessed=16 * tokens * width, transcendentals=heads * tokens * tokens
        ),
        name="hierarchical_attention",
    )(queries, key_states, value_states, out_grad)
    return pl.pallas_call(
        write_out,
        out_shape=[jax.ShapeDtypeStruct((tokens, width), BF16)] * 4,
        in_specs=[pl.BlockSpec(memory_space=pltpu.VMEM)] * 4,
        out_specs=[pl.BlockSpec(memory_space=pltpu.HBM)] * 4,
        scratch_shapes=[pltpu.SemaphoreType.DMA((4, PIECES))],
        compiler_params=pltpu.CompilerParams(vmem_limit_bytes=VMEM),
        name="write_out",
    )(*kept)


def solution(mesh):
    return jax.shard_map(
        shards,
        mesh=mesh,
        in_specs=(P("seq", "head"),) * 4,
        out_specs=(P("seq", "head"),) * 4,
        check_vma=False,
    )
```
